32 devices in a mesh: groups: 2 (over x), rows: 16 (over z, y, core).
Axes of the slice: x: 2, y: 2, z: 4, core: 2. Of those that a mesh axis runs over, the one named last changes fastest.
Arguments:
- occupied: bfloat16 [8192, 512], P(('groups', 'rows')), parts along dimension 0, may hold values from -6 to 6
- occupied_scale: float32 [1024], P('groups'), parts along dimension 0, may hold values from 0.013258252 to 0.13258252
- virtual: bfloat16 [8192, 512], P(('groups', 'rows')), parts along dimension 0, may hold values from -6 to 6
- virtual_scale: float32 [1024], P('groups'), parts along dimension 0, may hold values from 0.013258252 to 0.13258252
- trial: bfloat16 [8192, 512], P(('groups', 'rows')), parts along dimension 0, may hold values from -0.09375 to 0.09375
Outputs:
- applied: float32 [8192, 512], P(('groups', 'rows')), parts along dimension 0
The draws below stay inside these ranges and needn't reach their ends.
There are 2 independent parts, one for each index of `groups`. The reference program is written for one: setup_inputs(seed, part) draws one part's arguments, and reference() takes and returns one part's arrays. A program takes and returns all parts, laid end to end along the dimension named above; each array names one. Nothing has to cross between parts.
All inputs are finite; a program needn't handle non-finite values.
Results may differ from the reference program's by a relative error of at most 0.003.
Values may be sent and summed in bfloat16 or wider, within the bound.
A program may use at most 128 MiB of HBM per device.

```python
import math
import jax
import jax.numpy as jnp
from jax import lax

OCC = 512
VIR = 512
KTRIAL = 512
NP = 4096


def block_levels(rng, dims, cuts, smallest, largest):
    level, own = 1.0, jax.random.fold_in(rng, 6)
    for position, parts in cuts:
        heights = jnp.exp(jax.random.uniform(jax.random.fold_in(own, position), (parts,), jnp.float32, smallest / len(cuts), largest / len(cuts)))
        level = level * jnp.repeat(heights, dims[position] // parts).reshape([-1 if axis == position else 1 for axis in range(len(dims))])
    return level


def normal_values(rng, dims, width, most, shards=(), kind=jnp.bfloat16):
    array = width * jax.random.normal(rng, dims, jnp.float32)
    if shards:
        array = array * block_levels(rng, dims, shards, -0.22, 0.18)
    return jnp.clip(array, -most, most).astype(kind)


def setup_inputs(seed: int = 0, part: int = 0) -> dict:
    key_of = jax.random.split(jax.random.key(seed), 6)
    own_keys = jax.random.split(jax.random.fold_in(key_of[5], part), 6)
    occupied = normal_values(own_keys[0], (NP, OCC), 1.0, 6.0, ((0, 16),))
    occupied_scale = jnp.clip(jnp.exp(jax.random.uniform(own_keys[1], (OCC,), jnp.float32, math.log(0.013258252), math.log(0.13258252))), 0.013258252, 0.13258252)
    virtual = normal_values(own_keys[2], (NP, VIR), 1.0, 6.0, ((0, 16),))
    virtual_scale = jnp.clip(jnp.exp(jax.random.uniform(own_keys[3], (VIR,), jnp.float32, math.log(0.013258252), math.log(0.13258252))), 0.013258252, 0.13258252)
    trial = normal_values(own_keys[4], (NP, KTRIAL), NP ** -0.5, 0.09375, ((0, 16),))
    return dict(occupied=occupied, occupied_scale=occupied_scale, virtual=virtual, virtual_scale=virtual_scale, trial=trial)


def reference(occupied, occupied_scale, virtual, virtual_scale, trial):
    scaled_occupied = (occupied.astype(jnp.float32) * occupied_scale[None, :]).astype(jnp.bfloat16)
    scaled_virtual = (virtual.astype(jnp.float32) * virtual_scale[None, :]).astype(jnp.bfloat16)
    block_rows = min(512, NP)
    count = NP // block_rows

    def one_block(index):
        start = (index * block_rows).astype(jnp.int32)
        left_occ = lax.dynamic_slice_in_dim(scaled_occupied, start, block_rows, 0)
        left_vir = lax.dynamic_slice_in_dim(scaled_virtual, start, block_rows, 0)
        green_occ = lax.dot_general(left_occ, occupied, (((1,), (1,)), ((), ())), preferred_element_type=jnp.float32)
        green_vir = lax.dot_general(left_vir, virtual, (((1,), (1,)), ((), ())), preferred_element_type=jnp.float32)
        response = (green_occ * green_vir).astype(jnp.bfloat16)
        return jnp.dot(response, trial, preferred_element_type=jnp.float32)

    blocks = lax.map(one_block, jnp.arange(count, dtype=jnp.int32))
    return blocks.reshape(NP, trial.shape[1])
```

```python
import functools

import jax
import jax.numpy as jnp
from jax import lax
from jax.experimental import pallas as pl
from jax.experimental.pallas import tpu as pltpu
from jax.sharding import PartitionSpec as P

MESH = pl.DeviceIdType.MESH
NT = (((1,), (1,)), ((), ()))


def chip_columns(mesh):
    spots = {tuple(getattr(d, "coords", (0, 0, 0))[:2]) for d in mesh.devices[0].flat}
    return len(spots)


def kernel(chips, columns, occ_ref, os_ref, vir_ref, vs_ref, tri_ref, out_ref,
           buf, so, sv, ring_send, ring_recv, pair_send, pair_recv):
    group = lax.axis_index("groups")
    me = lax.axis_index("rows")
    core = lax.rem(me, 2)
    chip = me // 2
    half = buf.shape[-2]
    depth = chips // columns

    def place_of(q):
        if columns != 2:
            return q
        z, y = q // 2, lax.rem(q, 2)
        return z * (1 - y) + (2 * depth - 1 - z) * y

    def chip_at(p):
        if columns != 2:
            return p
        y = p // depth
        z = p * (1 - y) + (2 * depth - 1 - p) * y
        return z * 2 + y

    place = place_of(chip)
    after = chip_at(lax.rem(place + 1, chips)) * 2 + core
    before = chip_at(lax.rem(place + chips - 1, chips)) * 2 + core
    twin = chip * 2 + 1 - core

    barrier = pltpu.get_barrier_semaphore()
    for other in (after, before, twin):
        pl.semaphore_signal(barrier, inc=1, device_id=(group, other), device_id_type=MESH)

    own = []
    for a, ref in enumerate((occ_ref, vir_ref, tri_ref)):
        for d in range(2):
            copy = pltpu.make_async_copy(
                ref.at[pl.ds(d * half, half)], buf.at[a, d, place, core], ring_recv.at[a, d, 0])
            copy.start()
            own.append(copy)
    pl.semaphore_wait(barrier, 3)

    def slot_of(d, s):
        return lax.rem(place + (chips - s if d == 0 else s), chips)

    def ring_copy(a, d, s):
        block = buf.at[a, d, slot_of(d, s), core]
        return pltpu.make_async_remote_copy(
            src_ref=block, dst_ref=block, send_sem=ring_send.at[a, d, s],
            recv_sem=ring_recv.at[a, d, s + 1],
            device_id=(group, after if d == 0 else before), device_id_type=MESH)

    def pair_copy(a, d, s):
        block = buf.at[a, d, slot_of(d, s), core]
        return pltpu.make_async_remote_copy(
            src_ref=block, dst_ref=block, send_sem=pair_send.at[a, d, s],
            recv_sem=pair_recv.at[a, d, s],
            device_id=(group, twin), device_id_type=MESH)

    def arrived(a, d, s):
        block = buf.at[a, d, slot_of(d, s), core]
        pltpu.make_async_copy(block, block, ring_recv.at[a, d, s]).wait()

    def twin_arrived(a, d, s):
        block = buf.at[a, d, slot_of(d, s), 1 - core]
        pltpu.make_async_copy(block, block, pair_recv.at[a, d, s]).wait()

    def step(s, carry):
        for a in range(3):
            for d in range(2):
                arrived(a, d, s)

                @pl.when(s < chips - 1)
                def _():
                    ring_copy(a, d, s).start()

                pair_copy(a, d, s).start()

        @pl.when(s == 0)
        def _():
            so[...] = (occ_rows(0) * os_ref[...]).astype(jnp.bfloat16)
            sv[...] = (occ_rows(1) * vs_ref[...]).astype(jnp.bfloat16)
            out_ref[...] = jnp.zeros_like(out_ref)

        for d in range(2):
            for a in range(3):
                twin_arrived(a, d, s)
            slot = slot_of(d, s)
            rows = [buf[a, d, slot].reshape(2 * half, buf.shape[-1]) for a in range(3)]
            green_occ = lax.dot_general(so[...], rows[0], NT, preferred_element_type=jnp.float32)
            green_vir = lax.dot_general(sv[...], rows[1], NT, preferred_element_type=jnp.float32)
            response = (green_occ * green_vir).astype(jnp.bfloat16)
            out_ref[...] += jnp.dot(response, rows[2], preferred_element_type=jnp.float32)
        return carry

    def occ_rows(a):
        return jnp.concatenate([buf[a, d, place, core] for d in range(2)], axis=0).astype(jnp.float32)

    lax.fori_loop(0, chips, step, 0)

    def finish(s, carry):
        for a in range(3):
            for d in range(2):
                @pl.when(s < chips - 1)
                def _():
                    ring_copy(a, d, s).wait_send()

                pair_copy(a, d, s).wait_send()
        return carry

    lax.fori_loop(0, chips, finish, 0)


def local(chips, columns, occupied, occupied_scale, virtual, virtual_scale, trial):
    rows, width = occupied.shape
    any_space = pl.BlockSpec(memory_space=pl.ANY)
    vmem = pl.BlockSpec(memory_space=pltpu.VMEM)
    points = rows * 2 * chips
    sems = pltpu.SemaphoreType.DMA((3, 2, chips))
    return pl.pallas_call(
        functools.partial(kernel, chips, columns),
        out_shape=jax.ShapeDtypeStruct((rows, trial.shape[1]), jnp.float32),
        in_specs=[any_space, vmem, any_space, vmem, any_space],
        out_specs=vmem,
        scratch_shapes=[
            pltpu.VMEM((3, 2, chips, 2, rows // 2, width), jnp.bfloat16),
            pltpu.VMEM((rows, width), jnp.bfloat16),
            pltpu.VMEM((rows, width), jnp.bfloat16),
            sems, sems, sems, sems,
        ],
        compiler_params=pltpu.CompilerParams(
            collective_id=0, has_side_effects=True, vmem_limit_bytes=48 * 1024 * 1024),
        cost_estimate=pl.CostEstimate(
            flops=6 * rows * points * width, bytes_accessed=8 * rows * width, transcendentals=0),
    )(occupied, occupied_scale[None, :], virtual, virtual_scale[None, :], trial)


def solution(mesh):
    spread, scale = P(("groups", "rows"), None), P("groups")
    body = functools.partial(local, mesh.shape["rows"] // 2, chip_columns(mesh))
    return jax.shard_map(
        body, mesh=mesh, in_specs=(spread, scale, spread, scale, spread),
        out_specs=spread, check_vma=False)
```

```python
import functools

import jax
import jax.numpy as jnp
from jax import lax
from jax.experimental import pallas as pl
from jax.experimental.pallas import tpu as pltpu
from jax.sharding import PartitionSpec as P

MESH = pl.DeviceIdType.MESH
NT = (((1,), (1,)), ((), ()))


def chip_columns(mesh):
    spots = {tuple(getattr(d, "coords", (0, 0, 0))[:2]) for d in mesh.devices[0].flat}
    return len(spots)


def kernel(chips, columns, occ_ref, os_ref, vir_ref, vs_ref, tri_ref, out_ref,
           buf, scales, so, sv, ring_send, ring_recv, pair_send, pair_recv, scale_sem):
    group = lax.axis_index("groups")
    me = lax.axis_index("rows")
    core = lax.rem(me, 2)
    chip = me // 2
    half = buf.shape[-2]
    depth = chips // columns

    def place_of(q):
        if columns != 2:
            return q
        z, y = q // 2, lax.rem(q, 2)
        return z * (1 - y) + (2 * depth - 1 - z) * y

    def chip_at(p):
        if columns != 2:
            return p
        y = p // depth
        z = p * (1 - y) + (2 * depth - 1 - p) * y
        return z * 2 + y

    place = place_of(chip)
    after = chip_at(lax.rem(place + 1, chips)) * 2 + core
    before = chip_at(lax.rem(place + chips - 1, chips)) * 2 + core
    twin = chip * 2 + 1 - core

    barrier = pltpu.get_barrier_semaphore()
    for other in (after, before, twin):
        pl.semaphore_signal(barrier, inc=1, device_id=(group, other), device_id_type=MESH)

    for a, ref in enumerate((occ_ref, vir_ref, tri_ref)):
        for d in range(2):
            copy = pltpu.make_async_copy(
                ref.at[pl.ds(d * half, half)], buf.at[a, d, place, core], ring_recv.at[a, d, 0])
            copy.start()
    loads = [pltpu.make_async_copy(ref, scales.at[a], scale_sem.at[a]) for a, ref in enumerate((os_ref, vs_ref))]
    for copy in loads:
        copy.start()
    pl.semaphore_wait(barrier, 3)

    def slot_of(d, s):
        return lax.rem(place + (chips - s if d == 0 else s), chips)

    def ring_copy(a, d, s):
        block = buf.at[a, d, slot_of(d, s), core]
        return pltpu.make_async_remote_copy(
            src_ref=block, dst_ref=block, send_sem=ring_send.at[a, d, s],
            recv_sem=ring_recv.at[a, d, s + 1],
            device_id=(group, after if d == 0 else before), device_id_type=MESH)

    def pair_copy(a, d, s):
        block = buf.at[a, d, slot_of(d, s), core]
        return pltpu.make_async_remote_copy(
            src_ref=block, dst_ref=block, send_sem=pair_send.at[a, d, s],
            recv_sem=pair_recv.at[a, d, s],
            device_id=(group, twin), device_id_type=MESH)

    def arrived(a, d, s):
        block = buf.at[a, d, slot_of(d, s), core]
        pltpu.make_async_copy(block, block, ring_recv.at[a, d, s]).wait()

    def twin_arrived(a, d, s):
        block = buf.at[a, d, slot_of(d, s), 1 - core]
        pltpu.make_async_copy(block, block, pair_recv.at[a, d, s]).wait()

    def step(s, carry):
        for a in range(3):
            for d in range(2):
                arrived(a, d, s)

                @pl.when(s < chips - 1)
                def _():
                    ring_copy(a, d, s).start()

                pair_copy(a, d, s).start()

        @pl.when(s == 0)
        def _():
            for copy in loads:
                copy.wait()
            so[...] = (occ_rows(0) * scales[0]).astype(jnp.bfloat16)
            sv[...] = (occ_rows(1) * scales[1]).astype(jnp.bfloat16)
            out_ref[...] = jnp.zeros_like(out_ref)

        for d in range(2):
            for a in range(3):
                twin_arrived(a, d, s)
            slot = slot_of(d, s)
            rows = [buf[a, d, slot].reshape(2 * half, buf.shape[-1]) for a in range(3)]
            green_occ = lax.dot_general(so[...], rows[0], NT, preferred_element_type=jnp.float32)
            green_vir = lax.dot_general(sv[...], rows[1], NT, preferred_element_type=jnp.float32)
            response = (green_occ * green_vir).astype(jnp.bfloat16)
            out_ref[...] += jnp.dot(response, rows[2], preferred_element_type=jnp.float32)
        return carry

    def occ_rows(a):
        return jnp.concatenate([buf[a, d, place, core] for d in range(2)], axis=0).astype(jnp.float32)

    lax.fori_loop(0, chips, step, 0)

    def finish(s, carry):
        for a in range(3):
            for d in range(2):
                @pl.when(s < chips - 1)
                def _():
                    ring_copy(a, d, s).wait_send()

                pair_copy(a, d, s).wait_send()
        return carry

    lax.fori_loop(0, chips, finish, 0)


def local(chips, columns, occupied, occupied_scale, virtual, virtual_scale, trial):
    rows, width = occupied.shape
    any_space = pl.BlockSpec(memory_space=pl.ANY)
    vmem = pl.BlockSpec(memory_space=pltpu.VMEM)
    points = rows * 2 * chips
    sems = pltpu.SemaphoreType.DMA((3, 2, chips))
    return pl.pallas_call(
        functools.partial(kernel, chips, columns),
        out_shape=jax.ShapeDtypeStruct((rows, trial.shape[1]), jnp.float32),
        in_specs=[any_space] * 5,
        out_specs=vmem,
        scratch_shapes=[
            pltpu.VMEM((3, 2, chips, 2, rows // 2, width), jnp.bfloat16),
            pltpu.VMEM((2, 1, width), jnp.float32),
            pltpu.VMEM((rows, width), jnp.bfloat16),
            pltpu.VMEM((rows, width), jnp.bfloat16),
            sems, sems, sems, sems, pltpu.SemaphoreType.DMA((2,)),
        ],
        compiler_params=pltpu.CompilerParams(
            collective_id=0, has_side_effects=True, vmem_limit_bytes=60 * 1024 * 1024),
        cost_estimate=pl.CostEstimate(
            flops=6 * rows * points * width, bytes_accessed=8 * rows * width, transcendentals=0),
    )(occupied, occupied_scale[None, :], virtual, virtual_scale[None, :], trial)


def solution(mesh):
    spread, scale = P(("groups", "rows"), None), P("groups")
    body = functools.partial(local, mesh.shape["rows"] // 2, chip_columns(mesh))
    return jax.shard_map(
        body, mesh=mesh, in_specs=(spread, scale, spread, scale, spread),
        out_specs=spread, check_vma=False)
```

```python
import functools

import jax
import jax.numpy as jnp
from jax import lax
from jax.experimental import pallas as pl
from jax.experimental.pallas import tpu as pltpu
from jax.sharding import PartitionSpec as P

MESH = pl.DeviceIdType.MESH
NT = (((1,), (1,)), ((), ()))


def chip_columns(mesh):
    spots = {tuple(getattr(d, "coords", (0, 0, 0))[:2]) for d in mesh.devices[0].flat}
    return len(spots)


def kernel(chips, columns, occ_ref, os_ref, vir_ref, vs_ref, tri_ref, out_ref,
           buf, scales, so, sv, guest, part, back, came,
           ring_send, ring_recv, pair_send, pair_recv, back_send, back_recv, scale_sem):
    group = lax.axis_index("groups")
    me = lax.axis_index("rows")
    core = lax.rem(me, 2)
    chip = me // 2
    half = buf.shape[-2]
    reach = chips // 2
    depth = chips // columns

    def place_of(q):
        if columns != 2:
            return q
        z, y = q // 2, lax.rem(q, 2)
        return z * (1 - y) + (2 * depth - 1 - z) * y

    def chip_at(p):
        if columns != 2:
            return p
        y = p // depth
        z = p * (1 - y) + (2 * depth - 1 - p) * y
        return z * 2 + y

    place = place_of(chip)
    after = chip_at(lax.rem(place + 1, chips)) * 2 + core
    before = chip_at(lax.rem(place + chips - 1, chips)) * 2 + core
    twin = chip * 2 + 1 - core

    barrier = pltpu.get_barrier_semaphore()
    for other in (after, before, twin):
        pl.semaphore_signal(barrier, inc=1, device_id=(group, other), device_id_type=MESH)

    for a, ref in enumerate((occ_ref, vir_ref, tri_ref)):
        for d in range(2):
            copy = pltpu.make_async_copy(
                ref.at[pl.ds(d * half, half)], buf.at[a, d, place, core], ring_recv.at[a, d, 0])
            copy.start()
    loads = [pltpu.make_async_copy(ref, scales.at[a], scale_sem.at[a]) for a, ref in enumerate((os_ref, vs_ref))]
    for copy in loads:
        copy.start()
    pl.semaphore_wait(barrier, 3)

    def slot_of(d, s):
        return lax.rem(place + (chips - s if d == 0 else s), chips)

    def ring_copy(a, d, s):
        block = buf.at[a, d, slot_of(d, s), core]
        return pltpu.make_async_remote_copy(
            src_ref=block, dst_ref=block, send_sem=ring_send.at[a, d, s],
            recv_sem=ring_recv.at[a, d, s + 1],
            device_id=(group, after if d == 0 else before), device_id_type=MESH)

    def pair_copy(a, d, s):
        block = buf.at[a, d, slot_of(d, s), core]
        return pltpu.make_async_remote_copy(
            src_ref=block, dst_ref=block, send_sem=pair_send.at[a, d, s],
            recv_sem=pair_recv.at[a, d, s],
            device_id=(group, twin), device_id_type=MESH)

    def arrived(a, d, s):
        block = buf.at[a, d, slot_of(d, s), core]
        pltpu.make_async_copy(block, block, ring_recv.at[a, d, s]).wait()

    def twin_arrived(a, d, s):
        block = buf.at[a, d, slot_of(d, s), 1 - core]
        pltpu.make_async_copy(block, block, pair_recv.at[a, d, s]).wait()

    def scaled(a, rows):
        return (rows.astype(jnp.float32) * scales[a]).astype(jnp.bfloat16)

    def product(left_occ, left_vir, d, slot):
        rows = [buf[a, d, slot].reshape(2 * half, buf.shape[-1]) for a in range(3)]
        green_occ = lax.dot_general(left_occ, rows[0], NT, preferred_element_type=jnp.float32)
        green_vir = lax.dot_general(left_vir, rows[1], NT, preferred_element_type=jnp.float32)
        response = (green_occ * green_vir).astype(jnp.bfloat16)
        return jnp.dot(response, rows[2], preferred_element_type=jnp.float32)

    def receive(s, forward):
        for a in range(3):
            for d in range(2):
                arrived(a, d, s)
                if forward:
                    ring_copy(a, d, s).start()
                pair_copy(a, d, s).start()

    def receive_twin(s):
        for d in range(2):
            for a in range(3):
                twin_arrived(a, d, s)

    def step(s, carry):
        receive(s, True)

        @pl.when(s == 0)
        def _():
            for copy in loads:
                copy.wait()
            for d in range(2):
                so[pl.ds(d * half, half)] = scaled(0, buf[0, d, place, core])
                sv[pl.ds(d * half, half)] = scaled(1, buf[1, d, place, core])
            out_ref[...] = jnp.zeros_like(out_ref)

        @pl.when(s > 0)
        def _():
            for d in range(2):
                slot = slot_of(d, s)
                guest[d, s - 1, 0] = scaled(0, buf[0, d, slot, core])
                guest[d, s - 1, 1] = scaled(1, buf[1, d, slot, core])
                part[d, s - 1] = product(guest[d, s - 1, 0], guest[d, s - 1, 1], d, place)

        receive_twin(s)
        for d in range(2):
            out_ref[...] += product(so[...], sv[...], d, slot_of(d, s))
        return carry

    lax.fori_loop(0, reach, step, 0)
    receive(reach, False)
    receive_twin(reach)

    def back_copy(d, t):
        return pltpu.make_async_remote_copy(
            src_ref=back.at[d, t], dst_ref=came.at[d, t], send_sem=back_send.at[d, t],
            recv_sem=back_recv.at[d, t],
            device_id=(group, before if d == 0 else after), device_id_type=MESH)

    def stage(t, first):
        e = reach - 1 - t
        for d in range(2):
            total = part[d, e - 1] + product(
                guest[d, e - 1, 0], guest[d, e - 1, 1], 1 - d, slot_of(1 - d, reach))
            if not first:
                back_copy(d, t - 1).wait_recv()
                total += came[d, t - 1].astype(jnp.float32)
            back[d, t] = total.astype(jnp.bfloat16)
            back_copy(d, t).start()

    stage(0, True)
    for d in range(2):
        out_ref[...] += product(so[...], sv[...], d, slot_of(d, reach))

    def later_stage(t, carry):
        stage(t, False)
        return carry

    lax.fori_loop(1, reach - 1, later_stage, 0)
    for d in range(2):
        back_copy(d, reach - 2).wait_recv()
        out_ref[pl.ds(d * half, half)] += came[d, reach - 2].astype(jnp.float32)

    def finish(s, carry):
        for a in range(3):
            for d in range(2):
                @pl.when(s < reach)
                def _():
                    ring_copy(a, d, s).wait_send()

                pair_copy(a, d, s).wait_send()
        for d in range(2):
            @pl.when(s < reach - 1)
            def _():
                back_copy(d, s).wait_send()
        return carry

    lax.fori_loop(0, reach + 1, finish, 0)


def local(chips, columns, occupied, occupied_scale, virtual, virtual_scale, trial):
    rows, width = occupied.shape
    any_space = pl.BlockSpec(memory_space=pl.ANY)
    vmem = pl.BlockSpec(memory_space=pltpu.VMEM)
    points = rows * 2 * chips
    reach = chips // 2
    sems = pltpu.SemaphoreType.DMA((3, 2, reach + 1))
    back_sems = pltpu.SemaphoreType.DMA((2, reach - 1))
    back_rows = pltpu.VMEM((2, reach - 1, rows // 2, width), jnp.bfloat16)
    return pl.pallas_call(
        functools.partial(kernel, chips, columns),
        out_shape=jax.ShapeDtypeStruct((rows, trial.shape[1]), jnp.float32),
        in_specs=[any_space] * 5,
        out_specs=vmem,
        scratch_shapes=[
            pltpu.VMEM((3, 2, chips, 2, rows // 2, width), jnp.bfloat16),
            pltpu.VMEM((2, 1, width), jnp.float32),
            pltpu.VMEM((rows, width), jnp.bfloat16),
            pltpu.VMEM((rows, width), jnp.bfloat16),
            pltpu.VMEM((2, reach - 1, 2, rows // 2, width), jnp.bfloat16),
            pltpu.VMEM((2, reach - 1, rows // 2, width), jnp.float32),
            back_rows, back_rows,
            sems, sems, sems, sems, back_sems, back_sems, pltpu.SemaphoreType.DMA((2,)),
        ],
        compiler_params=pltpu.CompilerParams(
            collective_id=0, has_side_effects=True, vmem_limit_bytes=60 * 1024 * 1024),
        cost_estimate=pl.CostEstimate(
            flops=6 * rows * points * width, bytes_accessed=8 * rows * width, transcendentals=0),
    )(occupied, occupied_scale[None, :], virtual, virtual_scale[None, :], trial)


def solution(mesh):
    spread, scale = P(("groups", "rows"), None), P("groups")
    body = functools.partial(local, mesh.shape["rows"] // 2, chip_columns(mesh))
    return jax.shard_map(
        body, mesh=mesh, in_specs=(spread, scale, spread, scale, spread),
        out_specs=spread, check_vma=False)
```

```python
import functools

import jax
import jax.numpy as jnp
from jax import lax
from jax.experimental import pallas as pl
from jax.experimental.pallas import tpu as pltpu
from jax.sharding import PartitionSpec as P

MESH = pl.DeviceIdType.MESH
PIECES = 2
NT = (((1,), (1,)), ((), ()))


def chip_columns(mesh):
    spots = {tuple(getattr(d, "coords", (0, 0, 0))[:2]) for d in mesh.devices[0].flat}
    return len(spots)


def kernel(chips, columns, occ_ref, os_ref, vir_ref, vs_ref, tri_ref, out_ref,
           buf, scales, so, sv, guest, part, back, came,
           ring_send, ring_recv, pair_send, pair_recv, back_send, back_recv, scale_sem):
    group = lax.axis_index("groups")
    me = lax.axis_index("rows")
    core = lax.rem(me, 2)
    chip = me // 2
    half = buf.shape[-2]
    reach = chips // 2
    pieces, piece = back.shape[2], back.shape[-1]
    depth = chips // columns

    def place_of(q):
        if columns != 2:
            return q
        z, y = q // 2, lax.rem(q, 2)
        return z * (1 - y) + (2 * depth - 1 - z) * y

    def chip_at(p):
        if columns != 2:
            return p
        y = p // depth
        z = p * (1 - y) + (2 * depth - 1 - p) * y
        return z * 2 + y

    place = place_of(chip)
    after = chip_at(lax.rem(place + 1, chips)) * 2 + core
    before = chip_at(lax.rem(place + chips - 1, chips)) * 2 + core
    twin = chip * 2 + 1 - core

    barrier = pltpu.get_barrier_semaphore()
    for other in (after, before, twin):
        pl.semaphore_signal(barrier, inc=1, device_id=(group, other), device_id_type=MESH)

    for a, ref in enumerate((occ_ref, vir_ref, tri_ref)):
        for d in range(2):
            copy = pltpu.make_async_copy(
                ref.at[pl.ds(d * half, half)], buf.at[a, d, place, core], ring_recv.at[a, d, 0])
            copy.start()
    loads = [pltpu.make_async_copy(ref, scales.at[a], scale_sem.at[a]) for a, ref in enumerate((os_ref, vs_ref))]
    for copy in loads:
        copy.start()
    pl.semaphore_wait(barrier, 3)

    def slot_of(d, s):
        return lax.rem(place + (chips - s if d == 0 else s), chips)

    def ring_copy(a, d, s):
        block = buf.at[a, d, slot_of(d, s), core]
        return pltpu.make_async_remote_copy(
            src_ref=block, dst_ref=block, send_sem=ring_send.at[a, d, s],
            recv_sem=ring_recv.at[a, d, s + 1],
            device_id=(group, after if d == 0 else before), device_id_type=MESH)

    def pair_copy(a, d, s):
        block = buf.at[a, d, slot_of(d, s), core]
        return pltpu.make_async_remote_copy(
            src_ref=block, dst_ref=block, send_sem=pair_send.at[a, d, s],
            recv_sem=pair_recv.at[a, d, s],
            device_id=(group, twin), device_id_type=MESH)

    def arrived(a, d, s):
        block = buf.at[a, d, slot_of(d, s), core]
        pltpu.make_async_copy(block, block, ring_recv.at[a, d, s]).wait()

    def twin_arrived(a, d, s):
        block = buf.at[a, d, slot_of(d, s), 1 - core]
        pltpu.make_async_copy(block, block, pair_recv.at[a, d, s]).wait()

    def scaled(a, rows):
        return (rows.astype(jnp.float32) * scales[a]).astype(jnp.bfloat16)

    def product(left_occ, left_vir, d, slot):
        rows = [buf[a, d, slot].reshape(2 * half, buf.shape[-1]) for a in range(3)]
        green_occ = lax.dot_general(left_occ, rows[0], NT, preferred_element_type=jnp.float32)
        green_vir = lax.dot_general(left_vir, rows[1], NT, preferred_element_type=jnp.float32)
        response = (green_occ * green_vir).astype(jnp.bfloat16)
        return jnp.dot(response, rows[2], preferred_element_type=jnp.float32)

    def receive(s, forward):
        for a in range(3):
            for d in range(2):
                arrived(a, d, s)
                if forward:
                    ring_copy(a, d, s).start()
                pair_copy(a, d, s).start()

    def receive_twin(s):
        for d in range(2):
            for a in range(3):
                twin_arrived(a, d, s)

    def step(s, carry):
        receive(s, True)

        @pl.when(s == 0)
        def _():
            for copy in loads:
                copy.wait()
            for d in range(2):
                so[pl.ds(d * half, half)] = scaled(0, buf[0, d, place, core])
                sv[pl.ds(d * half, half)] = scaled(1, buf[1, d, place, core])
            out_ref[...] = jnp.zeros_like(out_ref)

        @pl.when(s > 0)
        def _():
            for d in range(2):
                slot = slot_of(d, s)
                guest[d, s - 1, 0] = scaled(0, buf[0, d, slot, core])
                guest[d, s - 1, 1] = scaled(1, buf[1, d, slot, core])
                part[d, s - 1] = product(guest[d, s - 1, 0], guest[d, s - 1, 1], d, place)

        receive_twin(s)
        for d in range(2):
            out_ref[...] += product(so[...], sv[...], d, slot_of(d, s))
        return carry

    lax.fori_loop(0, reach, step, 0)
    receive(reach, False)
    receive_twin(reach)

    def back_copy(d, t, c):
        return pltpu.make_async_remote_copy(
            src_ref=back.at[d, t, c], dst_ref=came.at[d, t, c], send_sem=back_send.at[d, t, c],
            recv_sem=back_recv.at[d, t, c],
            device_id=(group, before if d == 0 else after), device_id_type=MESH)

    def columns_of(c):
        return slice(c * piece, (c + 1) * piece)

    def complete(d, e):
        return part[d, e - 1] + product(
            guest[d, e - 1, 0], guest[d, e - 1, 1], 1 - d, slot_of(1 - d, reach))

    for d in range(2):
        total = complete(d, reach - 1)
        for c in range(pieces):
            back[d, 0, c] = total[:, columns_of(c)].astype(jnp.bfloat16)
            back_copy(d, 0, c).start()

    def complete_later(t, carry):
        for d in range(2):
            part[d, reach - 2 - t] = complete(d, reach - 1 - t)
        return carry

    lax.fori_loop(1, reach - 1, complete_later, 0)
    for d in range(2):
        out_ref[...] += product(so[...], sv[...], d, slot_of(d, reach))

    def later_stage(t, carry):
        for c in range(pieces):
            for d in range(2):
                back_copy(d, t - 1, c).wait_recv()
                total = part[d, reach - 2 - t, :, columns_of(c)] + came[d, t - 1, c].astype(jnp.float32)
                back[d, t, c] = total.astype(jnp.bfloat16)
                back_copy(d, t, c).start()
        return carry

    lax.fori_loop(1, reach - 1, later_stage, 0)
    for c in range(pieces):
        for d in range(2):
            back_copy(d, reach - 2, c).wait_recv()
            out_ref[pl.ds(d * half, half), columns_of(c)] += came[d, reach - 2, c].astype(jnp.float32)

    def finish(s, carry):
        for a in range(3):
            for d in range(2):
                @pl.when(s < reach)
                def _():
                    ring_copy(a, d, s).wait_send()

                pair_copy(a, d, s).wait_send()
        for d in range(2):
            @pl.when(s < reach - 1)
            def _():
                for c in range(pieces):
                    back_copy(d, s, c).wait_send()
        return carry

    lax.fori_loop(0, reach + 1, finish, 0)


def local(chips, columns, occupied, occupied_scale, virtual, virtual_scale, trial):
    rows, width = occupied.shape
    any_space = pl.BlockSpec(memory_space=pl.ANY)
    vmem = pl.BlockSpec(memory_space=pltpu.VMEM)
    points = rows * 2 * chips
    reach = chips // 2
    sems = pltpu.SemaphoreType.DMA((3, 2, reach + 1))
    back_sems = pltpu.SemaphoreType.DMA((2, reach - 1, PIECES))
    back_rows = pltpu.VMEM((2, reach - 1, PIECES, rows // 2, width // PIECES), jnp.bfloat16)
    return pl.pallas_call(
        functools.partial(kernel, chips, columns),
        out_shape=jax.ShapeDtypeStruct((rows, trial.shape[1]), jnp.float32),
        in_specs=[any_space] * 5,
        out_specs=vmem,
        scratch_shapes=[
            pltpu.VMEM((3, 2, chips, 2, rows // 2, width), jnp.bfloat16),
            pltpu.VMEM((2, 1, width), jnp.float32),
            pltpu.VMEM((rows, width), jnp.bfloat16),
            pltpu.VMEM((rows, width), jnp.bfloat16),
            pltpu.VMEM((2, reach - 1, 2, rows // 2, width), jnp.bfloat16),
            pltpu.VMEM((2, reach - 1, rows // 2, width), jnp.float32),
            back_rows, back_rows,
            sems, sems, sems, sems, back_sems, back_sems, pltpu.SemaphoreType.DMA((2,)),
        ],
        compiler_params=pltpu.CompilerParams(
            collective_id=0, has_side_effects=True, vmem_limit_bytes=60 * 1024 * 1024),
        cost_estimate=pl.CostEstimate(
            flops=6 * rows * points * width, bytes_accessed=8 * rows * width, transcendentals=0),
    )(occupied, occupied_scale[None, :], virtual, virtual_scale[None, :], trial)


def solution(mesh):
    spread, scale = P(("groups", "rows"), None), P("groups")
    body = functools.partial(local, mesh.shape["rows"] // 2, chip_columns(mesh))
    return jax.shard_map(
        body, mesh=mesh, in_specs=(spread, scale, spread, scale, spread),
        out_specs=spread, check_vma=False)
```

```python
import functools

import jax
import jax.numpy as jnp
from jax import lax
from jax.experimental import pallas as pl
from jax.experimental.pallas import tpu as pltpu
from jax.sharding import PartitionSpec as P

MESH = pl.DeviceIdType.MESH
PIECES = 4
NT = (((1,), (1,)), ((), ()))


def chip_columns(mesh):
    spots = {tuple(getattr(d, "coords", (0, 0, 0))[:2]) for d in mesh.devices[0].flat}
    return len(spots)


def kernel(chips, columns, occ_ref, os_ref, vir_ref, vs_ref, tri_ref, out_ref,
           buf, scales, so, sv, guest, part, back, came,
           ring_send, ring_recv, pair_send, pair_recv, back_send, back_recv, scale_sem):
    group = lax.axis_index("groups")
    me = lax.axis_index("rows")
    core = lax.rem(me, 2)
    chip = me // 2
    half = buf.shape[-2]
    reach = chips // 2
    pieces, piece = back.shape[2], back.shape[-1]
    depth = chips // columns

    def place_of(q):
        if columns != 2:
            return q
        z, y = q // 2, lax.rem(q, 2)
        return z * (1 - y) + (2 * depth - 1 - z) * y

    def chip_at(p):
        if columns != 2:
            return p
        y = p // depth
        z = p * (1 - y) + (2 * depth - 1 - p) * y
        return z * 2 + y

    place = place_of(chip)
    after = chip_at(lax.rem(place + 1, chips)) * 2 + core
    before = chip_at(lax.rem(place + chips - 1, chips)) * 2 + core
    twin = chip * 2 + 1 - core

    barrier = pltpu.get_barrier_semaphore()
    for other in (after, before, twin):
        pl.semaphore_signal(barrier, inc=1, device_id=(group, other), device_id_type=MESH)

    for a, ref in enumerate((occ_ref, vir_ref, tri_ref)):
        for d in range(2):
            copy = pltpu.make_async_copy(
                ref.at[pl.ds(d * half, half)], buf.at[a, d, place, core], ring_recv.at[a, d, 0])
            copy.start()
    loads = [pltpu.make_async_copy(ref, scales.at[a], scale_sem.at[a]) for a, ref in enumerate((os_ref, vs_ref))]
    for copy in loads:
        copy.start()
    pl.semaphore_wait(barrier, 3)

    def slot_of(d, s):
        return lax.rem(place + (chips - s if d == 0 else s), chips)

    def ring_copy(a, d, s):
        block = buf.at[a, d, slot_of(d, s), core]
        return pltpu.make_async_remote_copy(
            src_ref=block, dst_ref=block, send_sem=ring_send.at[a, d, s],
            recv_sem=ring_recv.at[a, d, s + 1],
            device_id=(group, after if d == 0 else before), device_id_type=MESH)

    def pair_copy(a, d, s):
        block = buf.at[a, d, slot_of(d, s), core]
        return pltpu.make_async_remote_copy(
            src_ref=block, dst_ref=block, send_sem=pair_send.at[a, d, s],
            recv_sem=pair_recv.at[a, d, s],
            device_id=(group, twin), device_id_type=MESH)

    def arrived(a, d, s):
        block = buf.at[a, d, slot_of(d, s), core]
        pltpu.make_async_copy(block, block, ring_recv.at[a, d, s]).wait()

    def twin_arrived(a, d, s):
        block = buf.at[a, d, slot_of(d, s), 1 - core]
        pltpu.make_async_copy(block, block, pair_recv.at[a, d, s]).wait()

    def scaled(a, rows):
        return (rows.astype(jnp.float32) * scales[a]).astype(jnp.bfloat16)

    def product(left_occ, left_vir, d, slot):
        rows = [buf[a, d, slot].reshape(2 * half, buf.shape[-1]) for a in range(3)]
        green_occ = lax.dot_general(left_occ, rows[0], NT, preferred_element_type=jnp.float32)
        green_vir = lax.dot_general(left_vir, rows[1], NT, preferred_element_type=jnp.float32)
        response = (green_occ * green_vir).astype(jnp.bfloat16)
        return jnp.dot(response, rows[2], preferred_element_type=jnp.float32)

    def receive(s, forward):
        for a in range(3):
            for d in range(2):
                arrived(a, d, s)
                if forward:
                    ring_copy(a, d, s).start()
                pair_copy(a, d, s).start()

    def receive_twin(s):
        for d in range(2):
            for a in range(3):
                twin_arrived(a, d, s)

    def step(s, carry):
        receive(s, True)

        @pl.when(s == 0)
        def _():
            for copy in loads:
                copy.wait()
            for d in range(2):
                so[pl.ds(d * half, half)] = scaled(0, buf[0, d, place, core])
                sv[pl.ds(d * half, half)] = scaled(1, buf[1, d, place, core])
            out_ref[...] = jnp.zeros_like(out_ref)

        @pl.when(s > 0)
        def _():
            for d in range(2):
                slot = slot_of(d, s)
                guest[d, s - 1, 0] = scaled(0, buf[0, d, slot, core])
                guest[d, s - 1, 1] = scaled(1, buf[1, d, slot, core])
                part[d, s - 1] = product(guest[d, s - 1, 0], guest[d, s - 1, 1], d, place)

        receive_twin(s)
        for d in range(2):
            out_ref[...] += product(so[...], sv[...], d, slot_of(d, s))
        return carry

    lax.fori_loop(0, reach, step, 0)
    receive(reach, False)
    receive_twin(reach)

    def back_copy(d, t, c):
        return pltpu.make_async_remote_copy(
            src_ref=back.at[d, t, c], dst_ref=came.at[d, t, c], send_sem=back_send.at[d, t, c],
            recv_sem=back_recv.at[d, t, c],
            device_id=(group, before if d == 0 else after), device_id_type=MESH)

    def columns_of(c):
        return slice(c * piece, (c + 1) * piece)

    def complete(d, e):
        return part[d, e - 1] + product(
            guest[d, e - 1, 0], guest[d, e - 1, 1], 1 - d, slot_of(1 - d, reach))

    for d in range(2):
        total = complete(d, reach - 1)
        for c in range(pieces):
            back[d, 0, c] = total[:, columns_of(c)].astype(jnp.bfloat16)
            back_copy(d, 0, c).start()

    def complete_later(t, carry):
        for d in range(2):
            part[d, reach - 2 - t] = complete(d, reach - 1 - t)
        return carry

    lax.fori_loop(1, reach - 1, complete_later, 0)
    for d in range(2):
        out_ref[...] += product(so[...], sv[...], d, slot_of(d, reach))

    def finish(s, carry):
        for a in range(3):
            for d in range(2):
                @pl.when(s < reach)
                def _():
                    ring_copy(a, d, s).wait_send()

                pair_copy(a, d, s).wait_send()
        return carry

    lax.fori_loop(0, reach + 1, finish, 0)

    def later_stage(t, carry):
        for c in range(pieces):
            for d in range(2):
                back_copy(d, t - 1, c).wait_recv()
                total = part[d, reach - 2 - t, :, columns_of(c)] + came[d, t - 1, c].astype(jnp.float32)
                back[d, t, c] = total.astype(jnp.bfloat16)
                back_copy(d, t, c).start()
        return carry

    lax.fori_loop(1, reach - 1, later_stage, 0)
    for c in range(pieces):
        for d in range(2):
            back_copy(d, reach - 2, c).wait_recv()
            out_ref[pl.ds(d * half, half), columns_of(c)] += came[d, reach - 2, c].astype(jnp.float32)

    def finish_back(t, carry):
        for d in range(2):
            for c in range(pieces):
                back_copy(d, t, c).wait_send()
        return carry

    lax.fori_loop(0, reach - 1, finish_back, 0)


def local(chips, columns, occupied, occupied_scale, virtual, virtual_scale, trial):
    rows, width = occupied.shape
    any_space = pl.BlockSpec(memory_space=pl.ANY)
    vmem = pl.BlockSpec(memory_space=pltpu.VMEM)
    points = rows * 2 * chips
    reach = chips // 2
    sems = pltpu.SemaphoreType.DMA((3, 2, reach + 1))
    back_sems = pltpu.SemaphoreType.DMA((2, reach - 1, PIECES))
    back_rows = pltpu.VMEM((2, reach - 1, PIECES, rows // 2, width // PIECES), jnp.bfloat16)
    return pl.pallas_call(
        functools.partial(kernel, chips, columns),
        out_shape=jax.ShapeDtypeStruct((rows, trial.shape[1]), jnp.float32),
        in_specs=[any_space] * 5,
        out_specs=vmem,
        scratch_shapes=[
            pltpu.VMEM((3, 2, chips, 2, rows // 2, width), jnp.bfloat16),
            pltpu.VMEM((2, 1, width), jnp.float32),
            pltpu.VMEM((rows, width), jnp.bfloat16),
            pltpu.VMEM((rows, width), jnp.bfloat16),
            pltpu.VMEM((2, reach - 1, 2, rows // 2, width), jnp.bfloat16),
            pltpu.VMEM((2, reach - 1, rows // 2, width), jnp.float32),
            back_rows, back_rows,
            sems, sems, sems, sems, back_sems, back_sems, pltpu.SemaphoreType.DMA((2,)),
        ],
        compiler_params=pltpu.CompilerParams(
            collective_id=0, has_side_effects=True, vmem_limit_bytes=60 * 1024 * 1024),
        cost_estimate=pl.CostEstimate(
            flops=6 * rows * points * width, bytes_accessed=8 * rows * width, transcendentals=0),
    )(occupied, occupied_scale[None, :], virtual, virtual_scale[None, :], trial)


def solution(mesh):
    spread, scale = P(("groups", "rows"), None), P("groups")
    body = functools.partial(local, mesh.shape["rows"] // 2, chip_columns(mesh))
    return jax.shard_map(
        body, mesh=mesh, in_specs=(spread, scale, spread, scale, spread),
        out_specs=spread, check_vma=False)
```
